768 devices in a mesh: px: 64 (over x, y, core), py: 12 (over z).
Axes of the slice: x: 4, y: 8, z: 12, core: 2. Of those that a mesh axis runs over, the one named last changes fastest.
Arguments:
- fields: float32 [6, 35, 786432], P(None, None, ('px', 'py')), may hold values from -6 to 6
- metric: float32 [3, 3, 786432], P(None, None, ('px', 'py')), may hold values from -6 to 6
- normals: float32 [3, 4, 786432], P(None, None, ('px', 'py')), may hold values from -1 to 1
- face_scale: float32 [4, 786432], P(None, ('px', 'py')), may hold values from 0.5 to 3
- permittivity: float32 [786432], P(('px', 'py')), may hold values from 1 to 8
- derivative: float32 [3, 35, 35], replicated, may hold values from -1 to 1
- face_interp: float32 [4, 15, 35], replicated, may hold values from -1 to 1
- lift: float32 [35, 60], replicated, may hold values from -0.75 to 0.75
- neighbor: int32 [64, 12, 4096], P('px', 'py'), may hold values from 0 to 4607, as said below
- levels: int32 [64, 12, 8], replicated, may hold values from 0 to 1, as said below
Outputs:
- rate: float32 [6, 35, 786432], P(None, None, ('px', 'py'))
The draws below stay inside these ranges and needn't reach their ends.
Inputs may be any that keep to these rules, and one draw needn't show every extreme that they name: `neighbor`: on every subdomain each code below 4096 pairs two distinct slots mutually; each code 4 * 1024 + d * 128 + j (d < 4, j < 128) appears exactly once on every subdomain, on a slot of an element of block j // 16. `levels`: at most 4 ones among the 8 blocks of one subdomain, reached on some subdomain.
All inputs are finite; a program needn't handle non-finite values.
Results may differ from the reference program's by a relative error of at most 0.0003.
Values sent between devices are 32-bit elements; how exact they have to be, the bound alone decides.
No kernel may reach another device: no remote copies, remote signals or barrier semaphores. Data moves between devices by JAX's collectives and lax.ppermute only.
A program may use at most 128 MiB of HBM per device.

```python
import math
import jax
import jax.numpy as jnp
from jax import lax

NP = 35
NFP = 15
BLK = 128
BFB = 16
NB = 8
MOSTF = 4
ELEMS = 786432
N_PX = 64
N_PY = 12


def draw_neighbor(key, part):
    key = jax.random.fold_in(key, 11)
    device_count = N_PX * N_PY
    elements = NB * BLK
    border = NB * BFB

    def one_device(subkey):
        block_key, pair_key = jax.random.split(subkey)
        local_order = jax.vmap(lambda inner: jax.random.permutation(inner, 4 * BLK))(jax.random.split(block_key, NB))
        face_index = local_order // BLK
        member = local_order % BLK
        slot_ids = face_index * elements + jnp.arange(NB, dtype=jnp.int32)[:, None] * BLK + member
        bounded = slot_ids[:, :4 * BFB]
        position = jnp.arange(4 * BFB, dtype=jnp.int32)
        side = position // BFB
        within = position % BFB
        labels = 4 * elements + side[None, :] * border + jnp.arange(NB, dtype=jnp.int32)[:, None] * BFB + within[None, :]
        remaining = jax.random.permutation(pair_key, slot_ids[:, 4 * BFB:].reshape(-1))
        first_half = remaining[0::2]
        second_half = remaining[1::2]
        result = jnp.zeros((4 * elements,), jnp.int32)
        result = result.at[bounded.reshape(-1)].set(labels.reshape(-1))
        result = result.at[first_half].set(second_half).at[second_half].set(first_half)
        return result
    return jax.vmap(one_device)(jax.random.split(key, device_count)).reshape(N_PX, N_PY, 4 * elements)


def draw_levels(key, part):
    key = jax.random.fold_in(key, 7)
    count_key, chosen_key, order_key = jax.random.split(key, 3)
    device_count = N_PX * N_PY
    counts = jax.random.randint(count_key, (device_count,), 0, MOSTF + 1)
    chosen = jax.random.randint(chosen_key, (), 0, device_count)
    counts = jnp.where(jnp.arange(device_count) == chosen, MOSTF, counts)
    orders = jax.vmap(lambda inner: jax.random.permutation(inner, NB))(jax.random.split(order_key, device_count))
    labels = (orders < counts[:, None]).astype(jnp.int32)
    return labels.reshape(N_PX, N_PY, NB)


def block_levels(own_key, dims, cuts, least, largest):
    factor_of, own = 1.0, jax.random.fold_in(own_key, 6)
    for dim, shards_of in cuts:
        steps = jnp.exp(jax.random.uniform(jax.random.fold_in(own, dim), (shards_of,), jnp.float32, least / len(cuts), largest / len(cuts)))
        factor_of = factor_of * jnp.repeat(steps, dims[dim] // shards_of).reshape([-1 if axis == dim else 1 for axis in range(len(dims))])
    return factor_of


def centred(rng, dims, deviation, reach, cuts=(), kind=jnp.bfloat16):
    values = deviation * jax.random.normal(rng, dims, jnp.float32)
    if cuts:
        values = values * block_levels(rng, dims, cuts, -0.22, 0.18)
    return jnp.clip(values, -reach, reach).astype(kind)


def setup_inputs(seed: int = 0) -> dict:
    key_of = jax.random.split(jax.random.key(seed), 11)
    return {
        "fields": centred(key_of[0], (6, NP, ELEMS), 1.0, 6.0, ((2, 768),), jnp.float32),
        "metric": centred(key_of[1], (3, 3, ELEMS), 2.0, 6.0, ((2, 768),), jnp.float32),
        "normals": jnp.clip(jax.random.uniform(key_of[2], (3, 4, ELEMS), jnp.float32, -1.0, 1.0) * block_levels(key_of[2], (3, 4, ELEMS), ((2, 768),), -0.4, 0.0), -1.0, 1.0),
        "face_scale": jnp.clip(jnp.exp(math.log(3.0) - 1.7917595 * jax.random.uniform(key_of[3], (4, ELEMS), jnp.float32) ** block_levels(key_of[3], (4, ELEMS), ((1, 768),), -0.2, 0.2)), 0.5, 3.0),
        "permittivity": jnp.clip(jnp.exp(math.log(8.0) - 2.0794415 * jax.random.uniform(key_of[4], (ELEMS,), jnp.float32) ** block_levels(key_of[4], (ELEMS,), ((0, 768),), -0.2, 0.2)), 1.0, 8.0),
        "derivative": centred(key_of[5], (3, NP, NP), NP ** -0.5, 1.0, (), jnp.float32),
        "face_interp": centred(key_of[6], (4, NFP, NP), NP ** -0.5, 1.0, (), jnp.float32),
        "lift": centred(key_of[7], (NP, 4 * NFP), (4 * NFP) ** -0.5, 0.75, (), jnp.float32),
        "neighbor": draw_neighbor(jax.random.fold_in(key_of[10], 71), 0),
        "levels": draw_levels(jax.random.fold_in(key_of[10], 71), 0),
    }


COARSE_STEP = 0.2
PRECISE = lax.Precision.HIGHEST


def face_traces(state, face_interp):
    components = state.shape[0]
    traces = jnp.einsum('fmn,cne->cmfe', face_interp, state, precision=PRECISE)
    return traces.reshape(components * traces.shape[1], traces.shape[2] * traces.shape[3])


def cross_product(normal, vector):
    return jnp.stack([normal[1] * vector[2] - normal[2] * vector[1],
                      normal[2] * vector[0] - normal[0] * vector[2],
                      normal[0] * vector[1] - normal[1] * vector[0]])


def apply_metric(metric, nodal_grad):
    return jnp.stack([metric[i, 0] * nodal_grad[0] + metric[i, 1] * nodal_grad[1] + metric[i, 2] * nodal_grad[2]
                      for i in range(3)])


def tendency(state, metric, normals, face_scale, permittivity, derivative, lift, face_codes, table, own_traces):
    elements = state.shape[2]
    node_count = state.shape[1]
    face_nodes = own_traces.shape[0] // 6
    nodal_grad = jnp.einsum('anm,cme->acne', derivative, state, precision=PRECISE)
    gradient = apply_metric(metric, nodal_grad)
    curl_h = jnp.stack([gradient[1, 5] - gradient[2, 4], gradient[2, 3] - gradient[0, 5], gradient[0, 4] - gradient[1, 3]])
    curl_e = jnp.stack([gradient[1, 2] - gradient[2, 1], gradient[2, 0] - gradient[0, 2], gradient[0, 1] - gradient[1, 0]])
    exterior = jnp.take(table, face_codes, axis=1)
    jump_all = (exterior - own_traces).reshape(6, face_nodes, 4, elements)
    normal = normals[:, None]
    jump_e = jump_all[:3]
    jump_h = jump_all[3:]
    dot_e = jnp.sum(normal * jump_e, axis=0)
    dot_h = jnp.sum(normal * jump_h, axis=0)
    flux_e = cross_product(normal, jump_h) + jump_e - dot_e * normal
    flux_h = jump_h - dot_h * normal - cross_product(normal, jump_e)
    flux_all = jnp.concatenate([flux_e, flux_h]) * (0.5 * face_scale)
    lifted = jnp.einsum('nfm,cmfe->cne', lift.reshape(node_count, 4, face_nodes), flux_all, precision=PRECISE)
    rate_e = (curl_h + lifted[:3]) / permittivity
    rate_h = lifted[3:] - curl_e
    return jnp.concatenate([rate_e, rate_h])


def outgoing_slots(face_codes, elements, border):
    spots = jnp.where(face_codes >= 4 * elements, face_codes - 4 * elements, 4 * border)
    return jnp.zeros((4 * border,), jnp.int32).at[spots].set(jnp.arange(4 * elements, dtype=jnp.int32), mode='drop')


def reference(fields, metric, normals, face_scale, permittivity, derivative, face_interp, lift, neighbor, levels):
    device_count = N_PX * N_PY
    elements = NB * BLK
    border = NB * BFB
    trace_rows = 6 * NFP

    def per_device(array):
        shaped = array.reshape(array.shape[:-1] + (device_count, elements))
        return jnp.moveaxis(shaped, -2, 0)

    start = per_device(fields)
    metric_all = per_device(metric)
    normal_all = per_device(normals)
    scale_all = per_device(face_scale)
    medium_all = per_device(permittivity)
    code_all = neighbor.reshape(device_count, 4 * elements)
    slot_all = jax.vmap(lambda codes_one: outgoing_slots(codes_one, elements, border))(code_all)
    fine = jnp.repeat(levels.reshape(device_count, NB), BLK, axis=1)[:, None, None, :] > 0

    def outgoing(items):
        state, slots_one = items
        return jnp.take(face_traces(state, face_interp), slots_one, axis=1)

    def incoming(outbound):
        grid = outbound.reshape(N_PX, N_PY, trace_rows, 4, border)
        zero_x = jnp.zeros_like(grid[:1])
        lower_x = jnp.concatenate([zero_x, grid[:-1]], axis=0)[:, :, :, 1]
        upper_x = jnp.concatenate([grid[1:], zero_x], axis=0)[:, :, :, 0]
        zero_y = jnp.zeros_like(grid[:, :1])
        lower_y = jnp.concatenate([zero_y, grid[:, :-1]], axis=1)[:, :, :, 3]
        upper_y = jnp.concatenate([grid[:, 1:], zero_y], axis=1)[:, :, :, 2]
        return jnp.stack([lower_x, upper_x, lower_y, upper_y], axis=3).reshape(device_count, trace_rows, 4 * border)

    def local_rate(items):
        state, metric_one, normal_one, scale_one, medium_one, codes_one, received = items
        own_traces = face_traces(state, face_interp)
        table = jnp.concatenate([own_traces, received], axis=1)
        return tendency(state, metric_one, normal_one, scale_one, medium_one, derivative, lift, codes_one, table, own_traces)

    state_all = start
    summed = None
    initial = None
    for substep in range(4):
        received = incoming(lax.map(outgoing, (state_all, slot_all)))
        change = lax.map(local_rate, (state_all, metric_all, normal_all, scale_all, medium_all, code_all, received))
        if substep == 0:
            initial = change
            summed = change
        else:
            summed = summed + change
        state_all = jnp.where(fine, state_all + (COARSE_STEP / 4) * change, start)
    rate = jnp.where(fine, summed * 0.25, initial)
    return jnp.moveaxis(rate, 0, -2).reshape(6, NP, device_count * elements)
```

```python
import jax
import jax.numpy as jnp
from jax import lax
from jax.experimental import pallas as pl
from jax.experimental.pallas import tpu as pltpu
from jax.sharding import PartitionSpec as P

F32 = jnp.float32
BF16 = jnp.bfloat16
BLK = 128
BFB = 16
NB = 8
NF = 4
NP = 35
NPAD = 40
KPAD = 48
FPAD = 16
STEP = 0.05
SLOTS = 4 * NB * BLK
FSLOTS = 4 * NF * BLK
FRECV = 4 * NF * BFB
ZROW = FSLOTS + FRECV
TAB = SLOTS + 4 * NB * BFB
FTAB = ZROW + 8
VMEM_LIMIT = 48 * 1024 * 1024


def split(x):
    hi = x.astype(BF16)
    lo = (x - hi.astype(F32)).astype(BF16)
    return hi, lo


def node_products(matrix, nodal):
    pad = jnp.zeros((KPAD - NPAD, 6 * BLK), F32)
    wide = jnp.concatenate([jnp.concatenate(nodal, axis=1), pad], axis=0)
    hi, lo = split(wide)
    return jnp.dot(matrix, jnp.concatenate([hi, lo, hi], axis=0), preferred_element_type=F32)


def store_traces(products, table, stride, base):
    for f in range(4):
        rows = products[f * FPAD : (f + 1) * FPAD]
        parts = [rows[:, c * BLK : (c + 1) * BLK] for c in range(6)]
        tile = jnp.concatenate(parts + [jnp.zeros((BLK - 6 * FPAD, BLK), F32)], axis=0)
        table[pl.ds(f * stride + base, BLK), :] = tile.T


def curls(products, metric, lanes):
    def nodal(a, c):
        return products[64 + a * NPAD : 64 + (a + 1) * NPAD, c * BLK : (c + 1) * BLK]

    rows = [[metric[i, a : a + 1, lanes] for a in range(3)] for i in range(3)]

    def grad(i, c):
        return rows[i][0] * nodal(0, c) + rows[i][1] * nodal(1, c) + rows[i][2] * nodal(2, c)

    curl_h = [grad(1, 5) - grad(2, 4), grad(2, 3) - grad(0, 5), grad(0, 4) - grad(1, 3)]
    curl_e = [grad(1, 2) - grad(2, 1), grad(2, 0) - grad(0, 2), grad(0, 1) - grad(1, 0)]
    return curl_h + curl_e


def cross(n, v):
    return [n[1] * v[2] - n[2] * v[1], n[2] * v[0] - n[0] * v[2], n[0] * v[1] - n[1] * v[0]]


def lifted_flux(outer, table, stride, base, normals, scale, lanes, lift):
    faces = [[], [], [], [], [], []]
    for f in range(4):
        at = pl.ds(f * stride + base, BLK)
        jump = (outer[at, :] - table[at, :]).T
        de = [jump[c * FPAD : (c + 1) * FPAD] for c in range(3)]
        dh = [jump[c * FPAD : (c + 1) * FPAD] for c in range(3, 6)]
        n = [normals[i, f : f + 1, lanes] for i in range(3)]
        half = 0.5 * scale[f : f + 1, lanes]
        dot_e = n[0] * de[0] + n[1] * de[1] + n[2] * de[2]
        dot_h = n[0] * dh[0] + n[1] * dh[1] + n[2] * dh[2]
        nh = cross(n, dh)
        ne = cross(n, de)
        for i in range(3):
            faces[i].append((nh[i] + de[i] - dot_e * n[i]) * half)
            faces[3 + i].append((dh[i] - dot_h * n[i] - ne[i]) * half)
    wide = jnp.concatenate([jnp.concatenate(x, axis=0) for x in faces], axis=1)
    hi, lo = split(wide)
    out = jnp.dot(lift, jnp.concatenate([hi, lo, hi], axis=0), preferred_element_type=F32)
    return [out[:NPAD, c * BLK : (c + 1) * BLK] for c in range(6)]


def tendency(curl, lifted, medium, lanes):
    inverse = 1.0 / medium[:, lanes]
    electric = [(curl[c] + lifted[c]) * inverse for c in range(3)]
    return electric + [lifted[c] - curl[c] for c in range(3, 6)]


def copy_rows(index, source, target, count, unroll):
    def body(g, _):
        base = pl.multiple_of(g * unroll, unroll)
        for r in range(unroll):
            target[pl.ds(base + r, 1), :] = source[pl.ds(index[base + r], 1), :]
        return 0

    lax.fori_loop(0, count // unroll, body, 0)


def send_rows(index, table, outs, width):
    for d in range(4):
        def body(g, _, d=d):
            base = pl.multiple_of(g * 16, 16)
            for r in range(16):
                outs[d][pl.ds(base + r, 1), :] = table[pl.ds(index[d * width + base + r], 1), :]
            return 0

        lax.fori_loop(0, width // 16, body, 0)


def pad_nodes(fields, padded):
    for c in range(6):
        padded[c, 32:NPAD, :] = jnp.zeros((NPAD - 32, NB * BLK), F32)
        padded[c, 0:NP, :] = fields[c]


def block_lanes(b):
    return pl.ds(pl.multiple_of(b * BLK, BLK), BLK)


def compact_rows(code, rank):
    inner_block = (code >> 7) & 7
    border = code - SLOTS
    outer_block = border >> 4
    inner_rank = jnp.full_like(code, NB)
    outer_rank = jnp.full_like(code, NB)
    for b in range(NB):
        inner_rank = jnp.where(inner_block == b, rank[b], inner_rank)
    for k in range(4 * NB):
        outer_rank = jnp.where(outer_block == k, rank[NB + k], outer_rank)
    inner = (code >> 10) * (NF * BLK) + inner_rank * BLK + (code & 127)
    outer = FSLOTS + (border >> 7) * (NF * BFB) + outer_rank * BFB + (border & 15)
    inner = jnp.where(inner_rank < NF, inner, ZROW)
    outer = jnp.where(outer_rank < NF, outer, ZROW)
    return jnp.where(code < SLOTS, inner, outer)


def first_kernel(slots, fields, front, out0, out1, out2, out3, padded, table):
    pad_nodes(fields, padded)
    for b in range(NB):
        lanes = pl.ds(b * BLK, BLK)
        products = node_products(front[0:64], [padded[c, :, lanes] for c in range(6)])
        store_traces(products, table, NB * BLK, b * BLK)
    send_rows(slots, table, [out0, out1, out2, out3], NB * BFB)


def full_kernel(
    codes, send, meta, rank, code_rows, fields, metric, normals, scale, medium, front, lift,
    in0, in1, in2, in3,
    rate, start, rows, out0, out1, out2, out3, padded, table, outer, curl, fine_table,
):
    for f in range(4):
        for i in range(NF):
            rows[f * NF + i : f * NF + i + 1, :] = code_rows[pl.ds(f * NB + meta[i], 1), :]
    rows[...] = compact_rows(rows[...], rank)
    pad_nodes(fields, padded)
    for d, got in enumerate((in0, in1, in2, in3)):
        table[SLOTS + d * NB * BFB : SLOTS + (d + 1) * NB * BFB, :] = got[...]
    for b in range(NB):
        lanes = pl.ds(b * BLK, BLK)
        products = node_products(front[...], [padded[c, :, lanes] for c in range(6)])
        store_traces(products, table, NB * BLK, b * BLK)
        for c, value in enumerate(curls(products, metric, lanes)):
            curl[b, c] = value
    copy_rows(codes, table, outer, SLOTS, 128)
    for b in range(NB):
        lanes = pl.ds(b * BLK, BLK)
        lifted = lifted_flux(outer, table, NB * BLK, b * BLK, normals, scale, lanes, lift[...])
        value = tendency([curl[b, c] for c in range(6)], lifted, medium, lanes)
        for c in range(6):
            curl[b, c] = value[c]
            rate[c, :, lanes] = value[c][:NP]
    for i in range(NF):
        keep = i < meta[NF]
        value = [jnp.where(keep, curl[meta[i], c], 0.0) for c in range(6)]
        for c in range(6):
            start[i, c] = value[c]
        store_traces(node_products(front[0:64], value), fine_table, NF * BLK, i * BLK)
    send_rows(send, fine_table, [out0, out1, out2, out3], NF * BFB)


def fine_update(
    codes, meta, state, start, metric, normals, scale, medium, front, lift, ins, table, outer, curl, emit
):
    for d, got in enumerate(ins):
        at = FSLOTS + d * NF * BFB
        table[at : at + NF * BFB, :] = got[...]
    table[ZROW : ZROW + 8, :] = jnp.zeros((8, BLK), F32)
    for i in range(NF):
        products = node_products(front[...], [state[i, c] for c in range(6)])
        store_traces(products, table, NF * BLK, i * BLK)
        for c, value in enumerate(curls(products, metric, block_lanes(meta[i]))):
            curl[i, c] = value
    copy_rows(codes, table, outer, FSLOTS, 128)
    for i in range(NF):
        lanes = block_lanes(meta[i])
        lifted = lifted_flux(outer, table, NF * BLK, i * BLK, normals, scale, lanes, lift[...])
        value = tendency([curl[i, c] for c in range(6)], lifted, medium, lanes)
        keep = i < meta[NF]
        emit(i, [
            jnp.where(keep, state[i, c] + start[i, c] + STEP * value[c], 0.0) for c in range(6)
        ])


def fine_kernel(
    codes, send, meta, state, start, metric, normals, scale, medium, front, lift, in0, in1, in2, in3,
    new_state, out0, out1, out2, out3, table, outer, curl,
):
    def emit(i, value):
        for c in range(6):
            new_state[i, c] = value[c]

    fine_update(
        codes, meta, state, start, metric, normals, scale, medium, front, lift,
        (in0, in1, in2, in3), table, outer, curl, emit,
    )
    for i in range(NF):
        products = node_products(front[0:64], [new_state[i, c] for c in range(6)])
        store_traces(products, table, NF * BLK, i * BLK)
    send_rows(send, table, [out0, out1, out2, out3], NF * BFB)


def last_kernel(
    codes, meta, state, start, metric, normals, scale, medium, front, lift, in0, in1, in2, in3, rate_in,
    rate, table, outer, curl, result, sem,
):
    def emit(i, value):
        for c in range(6):
            result[i, c] = value[c][:NP] * 0.25

    fine_update(
        codes, meta, state, start, metric, normals, scale, medium, front, lift,
        (in0, in1, in2, in3), table, outer, curl, emit,
    )

    def copy(i):
        return pltpu.make_async_copy(result.at[i], rate.at[:, :, block_lanes(meta[i])], sem.at[i])

    for i in range(NF):
        @pl.when(i < meta[NF])
        def _():
            copy(i).start()

    for i in range(NF):
        @pl.when(i < meta[NF])
        def _():
            copy(i).wait()


def border_slots(codes):
    per_block = codes.reshape(4, NB, BLK).transpose(1, 0, 2).reshape(NB, 1, 4 * BLK)
    side = lax.broadcasted_iota(jnp.int32, (NB, 4 * BFB, 1), 1)
    block = lax.broadcasted_iota(jnp.int32, (NB, 4 * BFB, 1), 0)
    wanted = SLOTS + (side // BFB) * (NB * BFB) + block * BFB + side % BFB
    place = lax.broadcasted_iota(jnp.int32, (NB, 1, 4 * BLK), 2)
    slot = (place // BLK) * (NB * BLK) + lax.broadcasted_iota(jnp.int32, (NB, 1, 4 * BLK), 0) * BLK + place % BLK
    found = jnp.sum(jnp.where(per_block == wanted, slot, 0), axis=2)
    return found.reshape(NB, 4, BFB).transpose(1, 0, 2)


def fine_plan(slots, levels):
    padded = jnp.pad(levels, ((1, 1), (1, 1), (0, 0)))
    near = lax.dynamic_slice(padded, (lax.axis_index("px"), lax.axis_index("py"), 0), (3, 3, NB))
    fine = (jnp.stack([near[1, 1], near[0, 1], near[2, 1], near[1, 0], near[1, 2]]) > 0).astype(jnp.int32)
    before = (jnp.arange(NB)[None, :] < jnp.arange(NB)[:, None]).astype(jnp.int32)
    fine_before = jnp.sum(fine[:, None, :] * before[None], axis=2)
    coarse_before = jnp.sum((1 - fine[:, None, :]) * before[None], axis=2)
    count = jnp.sum(fine, axis=1, keepdims=True)
    rank = jnp.where(fine > 0, fine_before, count + coarse_before)
    ids = jnp.arange(NB, dtype=jnp.int32)
    chosen = rank[0][None, :] == jnp.arange(NF)[:, None]
    order = jnp.sum(jnp.where(chosen, ids[None, :], 0), axis=1)
    meta = jnp.concatenate([order, count[0], jnp.zeros((3,), jnp.int32)])
    slot = jnp.sum(jnp.where(chosen[None, :, :, None], slots[:, None], 0), axis=2)
    send = (slot >> 10) * (NF * BLK) + jnp.arange(NF, dtype=jnp.int32)[None, :, None] * BLK + (slot & 127)
    return meta, rank.reshape(5 * NB), send.reshape(FRECV)


def stacked(matrix):
    hi = lax.reduce_precision(matrix, 8, 7)
    return jnp.concatenate([hi, hi, matrix - hi], axis=1).astype(BF16)


VMEM = pl.BlockSpec(memory_space=pltpu.VMEM)
SMEM = pl.BlockSpec(memory_space=pltpu.SMEM)
ANY = pl.BlockSpec(memory_space=pl.ANY)
PARAMS = pltpu.CompilerParams(vmem_limit_bytes=VMEM_LIMIT)


def cost(flops, size):
    return pl.CostEstimate(flops=flops, bytes_accessed=size, transcendentals=0)


def shards(
    fields, metric, normals, face_scale, permittivity, derivative, face_interp, lift, neighbor, levels
):
    codes = neighbor.reshape(4 * NB, BLK)
    medium = permittivity.reshape(1, NB * BLK)
    slots = border_slots(codes)
    front = jnp.concatenate([
        jnp.pad(face_interp, ((0, 0), (0, 1), (0, KPAD - NP))).reshape(4 * FPAD, KPAD),
        jnp.pad(derivative, ((0, 0), (0, NPAD - NP), (0, KPAD - NP))).reshape(3 * NPAD, KPAD),
        jnp.zeros((8, KPAD), F32),
    ])
    front = stacked(front)
    lift_wide = jnp.pad(lift.reshape(NP, 4, 15), ((0, KPAD - NP), (0, 0), (0, 1)))
    lift_wide = stacked(lift_wide.reshape(KPAD, 4 * FPAD))
    meta, rank, send = fine_plan(slots, levels)

    def exchange(out):
        def ways(axis):
            count = lax.axis_size(axis)
            return [(i, i + 1) for i in range(count - 1)], [(i + 1, i) for i in range(count - 1)]

        x_up, x_down = ways("px")
        y_up, y_down = ways("py")
        return (
            lax.ppermute(out[1], "px", x_up),
            lax.ppermute(out[0], "px", x_down),
            lax.ppermute(out[3], "py", y_up),
            lax.ppermute(out[2], "py", y_down),
        )

    def message(rows_of):
        return [jax.ShapeDtypeStruct((rows_of, BLK), F32)] * 4

    state_shape = jax.ShapeDtypeStruct((NF, 6, NPAD, BLK), F32)
    geometry = (metric, normals, face_scale, medium, front, lift_wide)
    out = pl.pallas_call(
        first_kernel,
        out_shape=message(NB * BFB),
        in_specs=[SMEM, VMEM, VMEM],
        out_specs=[VMEM] * 4,
        scratch_shapes=[pltpu.VMEM((6, NPAD, NB * BLK), F32), pltpu.VMEM((SLOTS, BLK), F32)],
        compiler_params=PARAMS,
        cost_estimate=cost(10**9, 2 * 10**6),
        name="border",
    )(slots.reshape(4 * NB * BFB), fields, front)
    received = exchange(out)
    rate, start, rows, *out = pl.pallas_call(
        full_kernel,
        out_shape=[
            jax.ShapeDtypeStruct((6, NP, NB * BLK), F32),
            state_shape,
            jax.ShapeDtypeStruct((4 * NF, BLK), jnp.int32),
        ] + message(NF * BFB),
        in_specs=[SMEM] * 4 + [VMEM] * 12,
        out_specs=[VMEM] * 7,
        scratch_shapes=[
            pltpu.VMEM((6, NPAD, NB * BLK), F32),
            pltpu.VMEM((TAB, BLK), F32),
            pltpu.VMEM((SLOTS, BLK), F32),
            pltpu.VMEM((NB, 6, NPAD, BLK), F32),
            pltpu.VMEM((FSLOTS, BLK), F32),
        ],
        compiler_params=PARAMS,
        cost_estimate=cost(10**9, 4 * 10**6),
        name="full",
    )(neighbor.reshape(SLOTS), send, meta, rank, codes, fields, *geometry, *received)
    rows = rows.reshape(FSLOTS)
    work = [
        pltpu.VMEM((FTAB, BLK), F32),
        pltpu.VMEM((FSLOTS, BLK), F32),
        pltpu.VMEM((NF, 6, NPAD, BLK), F32),
    ]
    state = start
    for _ in range(2):
        received = exchange(out)
        state, *out = pl.pallas_call(
            fine_kernel,
            out_shape=[state_shape] + message(NF * BFB),
            in_specs=[SMEM] * 3 + [VMEM] * 12,
            out_specs=[VMEM] * 5,
            scratch_shapes=work,
            compiler_params=PARAMS,
            cost_estimate=cost(10**9, 2 * 10**6),
            name="fine",
        )(rows, send, meta, state, start, *geometry, *received)
    received = exchange(out)
    return pl.pallas_call(
        last_kernel,
        out_shape=jax.ShapeDtypeStruct((6, NP, NB * BLK), F32),
        in_specs=[SMEM] * 2 + [VMEM] * 12 + [ANY],
        out_specs=ANY,
        scratch_shapes=work + [pltpu.VMEM((NF, 6, NP, BLK), F32), pltpu.SemaphoreType.DMA((NF,))],
        input_output_aliases={14: 0},
        compiler_params=PARAMS,
        cost_estimate=cost(10**9, 2 * 10**6),
        name="last",
    )(rows, meta, state, start, *geometry, *received, rate)


def solution(mesh):
    in_specs = (
        P(None, None, ("px", "py")),
        P(None, None, ("px", "py")),
        P(None, None, ("px", "py")),
        P(None, ("px", "py")),
        P(("px", "py")),
        P(),
        P(),
        P(),
        P("px", "py", None),
        P(),
    )
    out_specs = P(None, None, ("px", "py"))
    return jax.shard_map(shards, mesh=mesh, in_specs=in_specs, out_specs=out_specs, check_vma=False)
```

```python
import jax
import jax.numpy as jnp
from jax import lax
from jax.experimental import pallas as pl
from jax.experimental.pallas import tpu as pltpu
from jax.sharding import PartitionSpec as P

F32 = jnp.float32
BF16 = jnp.bfloat16
BLK = 128
BFB = 16
NB = 8
NF = 4
NP = 35
NPAD = 40
KLIFT = 48
KROWS = 128
FPAD = 16
STEP = 0.05
SLOTS = 4 * NB * BLK
FSLOTS = 4 * NF * BLK
FRECV = 4 * NF * BFB
ZROW = FSLOTS
TAB = SLOTS + 4 * NB * BFB
FTAB = ZROW + 8
TRASH = FSLOTS
VMEM_LIMIT = 16 * 1024 * 1024


def split(x):
    hi = x.astype(BF16)
    lo = (x - hi.astype(F32)).astype(BF16)
    return hi, lo


def node_products(matrix, nodal):
    wide = jnp.concatenate(nodal, axis=1)
    hi = wide.astype(BF16).astype(F32)
    zero = jnp.zeros((KROWS - 3 * NPAD, 6 * BLK), F32)
    wide = jnp.concatenate([hi, wide - hi, hi, zero], axis=0).astype(BF16)
    return jnp.dot(matrix, wide, preferred_element_type=F32)


def stacked(matrix):
    hi = matrix.astype(BF16).astype(F32)
    return (hi + pltpu.roll(hi, NPAD, 1) + pltpu.roll(matrix - hi, 2 * NPAD, 1)).astype(BF16)


def store_traces(products, table, stride, base):
    for f in range(4):
        rows = products[f * FPAD : (f + 1) * FPAD]
        parts = [rows[:, c * BLK : (c + 1) * BLK] for c in range(6)]
        tile = jnp.concatenate(parts + [jnp.zeros((BLK - 6 * FPAD, BLK), F32)], axis=0)
        table[pl.ds(f * stride + base, BLK), :] = tile.T


def curls(products, metric, lanes):
    def nodal(a, c):
        return products[a * NPAD : (a + 1) * NPAD, c * BLK : (c + 1) * BLK]

    rows = [[metric[i, a : a + 1, lanes] for a in range(3)] for i in range(3)]

    def grad(i, c):
        return rows[i][0] * nodal(0, c) + rows[i][1] * nodal(1, c) + rows[i][2] * nodal(2, c)

    curl_h = [grad(1, 5) - grad(2, 4), grad(2, 3) - grad(0, 5), grad(0, 4) - grad(1, 3)]
    curl_e = [grad(1, 2) - grad(2, 1), grad(2, 0) - grad(0, 2), grad(0, 1) - grad(1, 0)]
    return curl_h + curl_e


def cross(n, v):
    return [n[1] * v[2] - n[2] * v[1], n[2] * v[0] - n[0] * v[2], n[0] * v[1] - n[1] * v[0]]


def lifted_flux(outer, table, stride, base, normals, scale, lanes, lift):
    faces = [[], [], [], [], [], []]
    for f in range(4):
        at = pl.ds(f * stride + base, BLK)
        jump = (outer[at, :] - table[at, :]).T
        de = [jump[c * FPAD : (c + 1) * FPAD] for c in range(3)]
        dh = [jump[c * FPAD : (c + 1) * FPAD] for c in range(3, 6)]
        n = [normals[i, f : f + 1, lanes] for i in range(3)]
        half = 0.5 * scale[f : f + 1, lanes]
        dot_e = n[0] * de[0] + n[1] * de[1] + n[2] * de[2]
        dot_h = n[0] * dh[0] + n[1] * dh[1] + n[2] * dh[2]
        nh = cross(n, dh)
        ne = cross(n, de)
        for i in range(3):
            faces[i].append((nh[i] + de[i] - dot_e * n[i]) * half)
            faces[3 + i].append((dh[i] - dot_h * n[i] - ne[i]) * half)
    wide = jnp.concatenate([jnp.concatenate(x, axis=0) for x in faces], axis=1)
    hi, lo = split(wide)
    out = jnp.dot(lift[:, : 12 * FPAD], jnp.concatenate([hi, lo, hi], axis=0), preferred_element_type=F32)
    return [out[:NPAD, c * BLK : (c + 1) * BLK] for c in range(6)]


def tendency(curl, lifted, medium, lanes):
    inverse = 1.0 / medium[:, lanes]
    electric = [(curl[c] + lifted[c]) * inverse for c in range(3)]
    return electric + [lifted[c] - curl[c] for c in range(3, 6)]


def copy_rows(index, source, target, base):
    for r in range(BLK):
        target[pl.ds(base + r, 1), :] = source[pl.ds(index[base + r], 1), :]


def send_rows(index, table, outs):
    for d in range(4):
        for i in range(NF):
            for w in range(BFB):
                r = i * BFB + w
                outs[d][r : r + 1, :] = table[pl.ds(index[i, d * BFB + w], 1), :]


def pad_nodes(fields, padded, lo, hi):
    for c in range(6):
        padded[c, 32:NPAD, lo:hi] = jnp.zeros((NPAD - 32, hi - lo), F32)
        padded[c, 0:NP, lo:hi] = fields[c, :, lo:hi]


def block_lanes(b):
    return pl.ds(b * BLK if isinstance(b, int) else pl.multiple_of(b * BLK, BLK), BLK)


def each(count, body):
    for b in range(count):
        body(b)


def compact_rows(code, rank):
    block = (code >> 7) & 7
    place = jnp.full_like(code, NB)
    for b in range(NB):
        place = jnp.where(block == b, rank[0, b], place)
    row = (code >> 10) * (NF * BLK) + place * BLK + (code & 127)
    return jnp.where((code < SLOTS) & (place < NF), row, ZROW)


def find_slots(codes, wide, index):
    wide[...] = jnp.zeros_like(wide)
    wide[0 : 4 * NB, :] = codes[...].astype(F32)
    columns = wide[...].T
    lane = lax.broadcasted_iota(jnp.int32, (BLK, BLK), 1)
    element = lax.broadcasted_iota(jnp.int32, (BLK, BLK), 0).astype(F32)
    for b in range(NB):
        wanted = (SLOTS + (lane >> 4) * (NB * BFB) + b * BFB + (lane & 15)).astype(F32)
        found = jnp.zeros((BLK, BLK), F32)
        for f in range(4):
            column = columns[:, f * NB + b : f * NB + b + 1]
            found += jnp.where(column == wanted, element + (f * NB + b) * BLK, 0.0)
        index[b : b + 1, :] = jnp.sum(found, axis=0, keepdims=True).astype(jnp.int32)


def first_kernel(
    code_rows, fields, interp, slots, table, front, out0, out1, out2, out3,
    padded, raw, code_buf, interp_buf, wide, index, sem,
):
    half = NB * BLK // 2
    copies = [
        pltpu.make_async_copy(code_rows, code_buf, sem.at[0]),
        pltpu.make_async_copy(interp, interp_buf, sem.at[1]),
    ] + [
        pltpu.make_async_copy(
            fields.at[:, :, h * half : (h + 1) * half], raw.at[:, :, h * half : (h + 1) * half], sem.at[2 + h]
        )
        for h in range(2)
    ]
    for copy in copies:
        copy.start()
    table[SLOTS:TAB, :] = jnp.zeros((TAB - SLOTS, BLK), F32)
    copies[0].wait()
    find_slots(code_buf, wide, slots)
    to_scalar = pltpu.make_async_copy(slots, index, sem.at[4])
    to_scalar.start()
    copies[1].wait()
    wide[...] = jnp.zeros_like(wide)
    for f in range(4):
        for m in range(15):
            wide[f * FPAD + m : f * FPAD + m + 1, 0:NP] = interp_buf[m, f : f + 1, :]
    front[...] = stacked(wide[0 : 4 * FPAD, :])
    for h in range(2):
        copies[2 + h].wait()
        pad_nodes(raw, padded, h * half, (h + 1) * half)

        def traces(i, h=h):
            b = i + h * NB // 2
            lanes = block_lanes(b)
            products = node_products(front[...], [padded[c, :, lanes] for c in range(6)])
            store_traces(products, table, NB * BLK, b * BLK)

        each(NB // 2, traces)
    to_scalar.wait()
    for d, out in enumerate((out0, out1, out2, out3)):
        for b in range(NB):
            for w in range(BFB):
                out[b * BFB + w : b * BFB + w + 1, :] = table[pl.ds(index[b, d * BFB + w], 1), :]


def volume_kernel(
    codes, rank, code_rows, slots, table, fields, metric, derivative, lift,
    meta, outer, curl, rows, send, place, back, lift_wide, wide, padded, order,
):
    count = 0
    for x in range(5):
        for b in range(NB):
            order[x, rank[x, b]] = b
    for b in range(NB):
        meta[b] = order[0, b]
        count += rank[5, b]
    meta[NB] = count
    for f in range(4):
        for i in range(NF):
            rows[f * NF + i : f * NF + i + 1, :] = code_rows[pl.ds(f * NB + meta[i], 1), :]
    rows[...] = compact_rows(rows[...], rank)
    for i in range(NF):
        slot = slots[pl.ds(meta[i], 1), :]
        send[i : i + 1, :] = (slot >> 10) * (NF * BLK) + i * BLK + (slot & 127)
    for d in range(4):
        for i in range(NF):
            b = order[1 + d, i]
            own = rank[0, b]
            slot = slots[pl.ds(b, 1), :]
            row = (slot >> 10) * (NF * BLK) + own * BLK + (slot & 127)
            place[d * NF + i : d * NF + i + 1, :] = jnp.where(own < NF, row, TRASH)
    wide[...] = jnp.zeros_like(wide)
    for a in range(3):
        wide[a * NPAD : a * NPAD + NP, 0:NP] = derivative[a]
    back[...] = stacked(wide[...])
    wide[0:KLIFT, :] = jnp.zeros((KLIFT, BLK), F32)
    wide[0:NP, 0:60] = lift[...]
    flat = wide[0:KLIFT, :]
    lane = lax.broadcasted_iota(jnp.int32, (KLIFT, BLK), 1)
    face_major = jnp.where(lane < 15, flat, 0.0)
    for f in range(1, 4):
        inside = (lane >= f * FPAD) & (lane < f * FPAD + 15)
        face_major = jnp.where(inside, pltpu.roll(flat, f, 1), face_major)
    hi = face_major.astype(BF16).astype(F32)
    lift_wide[:, 0:BLK] = (hi + pltpu.roll(hi, 4 * FPAD, 1)).astype(BF16)
    lift_wide[:, BLK : 2 * BLK] = (face_major - hi).astype(BF16)
    pad_nodes(fields, padded, 0, NB * BLK)

    def block(b):
        lanes = block_lanes(b)
        for f in range(4):
            copy_rows(codes, table, outer, f * NB * BLK + b * BLK)
        products = node_products(back[...], [padded[c, :, lanes] for c in range(6)])
        for c, value in enumerate(curls(products, metric, lanes)):
            curl[b, c] = value

    each(NB, block)


def full_kernel(
    slots, send, meta, table, outer_in, curl, normals, scale, medium, front, lift, in0, in1, in2, in3,
    rate, start, fine_table, out0, out1, out2, out3, outer, result, value_all, sem,
):
    for d, got in enumerate((in0, in1, in2, in3)):
        for b in range(NB):
            for w in range(BFB):
                outer[pl.ds(slots[b, d * BFB + w], 1), :] = got[b * BFB + w : b * BFB + w + 1, :]
    def copy(b):
        return pltpu.make_async_copy(result.at[b], rate.at[:, :, block_lanes(b)], sem.at[b])

    def block(b):
        lanes = block_lanes(b)
        lifted = lifted_flux(outer, table, NB * BLK, b * BLK, normals, scale, lanes, lift)
        value = tendency([curl[b, c] for c in range(6)], lifted, medium, lanes)
        for c in range(6):
            value_all[b, c] = value[c]
            result[b, c] = value[c][:NP]
        copy(b).start()

    each(NB, block)
    fine_table[ZROW : ZROW + 8, :] = jnp.zeros((8, BLK), F32)

    def fine_block(i):
        keep = i < meta[NB]
        value = [jnp.where(keep, value_all[meta[i], c], 0.0) for c in range(6)]
        for c in range(6):
            start[i, c] = value[c]
        store_traces(node_products(front[...], value), fine_table, NF * BLK, i * BLK)

    each(NF, fine_block)
    send_rows(send, fine_table, (out0, out1, out2, out3))
    for b in range(NB):
        copy(b).wait()


def fine_volume_kernel(codes, meta, table, state, metric, back, outer, curl):
    def block(i):
        for f in range(4):
            copy_rows(codes, table, outer, f * NF * BLK + i * BLK)
        products = node_products(back[...], [state[i, c] for c in range(6)])
        for c, value in enumerate(curls(products, metric, block_lanes(meta[i]))):
            curl[i, c] = value

    each(NF, block)


def fine_update(
    place, meta, state, start, table, outer, curl, normals, scale, medium, lift, ins, emit
):
    for d, got in enumerate(ins):
        for i in range(NF):
            for w in range(BFB):
                r = i * BFB + w
                outer[pl.ds(place[d * NF + i, d * BFB + w], 1), :] = got[r : r + 1, :]
    def block(i):
        lanes = block_lanes(meta[i])
        lifted = lifted_flux(outer, table, NF * BLK, i * BLK, normals, scale, lanes, lift)
        value = tendency([curl[i, c] for c in range(6)], lifted, medium, lanes)
        keep = i < meta[NB]
        emit(i, [
            jnp.where(keep, state[i, c] + start[i, c] + STEP * value[c], 0.0) for c in range(6)
        ])

    each(NF, block)


def fine_kernel(
    place, send, meta, state, start, table, outer_in, curl, normals, scale, medium, front, lift,
    in0, in1, in2, in3, new_state, new_table, out0, out1, out2, out3, outer,
):
    def emit(i, value):
        for c in range(6):
            new_state[i, c] = value[c]
        store_traces(node_products(front[...], value), new_table, NF * BLK, i * BLK)

    new_table[ZROW : ZROW + 8, :] = jnp.zeros((8, BLK), F32)
    fine_update(
        place, meta, state, start, table, outer, curl, normals, scale, medium, lift,
        (in0, in1, in2, in3), emit,
    )
    send_rows(send, new_table, (out0, out1, out2, out3))


def last_kernel(
    place, meta, state, start, table, outer_in, curl, normals, scale, medium, lift,
    in0, in1, in2, in3, rate_in, rate, outer, result, sem,
):
    def copy(i):
        return pltpu.make_async_copy(result.at[i], rate.at[:, :, block_lanes(meta[i])], sem.at[i])

    def emit(i, value):
        for c in range(6):
            result[i, c] = value[c][:NP] * 0.25

        @pl.when(i < meta[NB])
        def _():
            copy(i).start()

    fine_update(
        place, meta, state, start, table, outer, curl, normals, scale, medium, lift,
        (in0, in1, in2, in3), emit,
    )
    for i in range(NF):
        @pl.when(i < meta[NB])
        def _():
            copy(i).wait()


def fine_plan(levels):
    padded = jnp.pad(levels, ((1, 1), (1, 1), (0, 0)))
    near = lax.dynamic_slice(padded, (lax.axis_index("px"), lax.axis_index("py"), 0), (3, 3, NB))
    fine = (jnp.stack([near[1, 1], near[0, 1], near[2, 1], near[1, 0], near[1, 2]]) > 0).astype(jnp.int32)
    before = (jnp.arange(NB)[None, :] < jnp.arange(NB)[:, None]).astype(jnp.int32)
    fine_before = jnp.sum(fine[:, None, :] * before[None], axis=2)
    coarse_before = jnp.sum((1 - fine[:, None, :]) * before[None], axis=2)
    count = jnp.sum(fine, axis=1, keepdims=True)
    rank = jnp.where(fine > 0, fine_before, count + coarse_before)
    return jnp.concatenate([rank, fine[:1]])


VMEM = pl.BlockSpec(memory_space=pltpu.VMEM)
SMEM = pl.BlockSpec(memory_space=pltpu.SMEM)
HBM = pl.BlockSpec(memory_space=pltpu.HBM)
PARAMS = pltpu.CompilerParams(vmem_limit_bytes=VMEM_LIMIT)


def cost(flops, size):
    return pl.CostEstimate(flops=flops, bytes_accessed=size, transcendentals=0)


def shards(
    fields, metric, normals, face_scale, permittivity, derivative, face_interp, lift, neighbor, levels
):
    codes = neighbor.reshape(4 * NB, BLK)
    medium = permittivity.reshape(1, NB * BLK)

    def exchange(out):
        def ways(axis):
            count = lax.axis_size(axis)
            return [(i, i + 1) for i in range(count - 1)], [(i + 1, i) for i in range(count - 1)]

        x_up, x_down = ways("px")
        y_up, y_down = ways("py")
        return (
            lax.ppermute(out[1], "px", x_up),
            lax.ppermute(out[0], "px", x_down),
            lax.ppermute(out[3], "py", y_up),
            lax.ppermute(out[2], "py", y_down),
        )

    def message(rows_of):
        return [jax.ShapeDtypeStruct((rows_of, BLK), F32)] * 4

    def array(*shape, dtype=F32):
        return jax.ShapeDtypeStruct(shape, dtype)

    state_shape = array(NF, 6, NPAD, BLK)
    ranks = fine_plan(levels)
    slots, table, front, *out = pl.pallas_call(
        first_kernel,
        out_shape=[
            array(NB, BLK, dtype=jnp.int32),
            array(TAB, BLK),
            array(4 * FPAD, KROWS, dtype=BF16),
        ] + message(NB * BFB),
        in_specs=[HBM] * 3,
        out_specs=[VMEM] * 7,
        scratch_shapes=[
            pltpu.VMEM((6, NPAD, NB * BLK), F32),
            pltpu.VMEM((6, NP, NB * BLK), F32),
            pltpu.VMEM((4 * NB, BLK), jnp.int32),
            pltpu.VMEM((15, 4, NP), F32),
            pltpu.VMEM((BLK, BLK), F32),
            pltpu.SMEM((NB, BLK), jnp.int32),
            pltpu.SemaphoreType.DMA((5,)),
        ],
        compiler_params=PARAMS,
        cost_estimate=cost(10**9, 2 * 10**6),
        name="border",
    )(codes, fields, face_interp.transpose(1, 0, 2))
    received = exchange(out)
    meta, outer, curl, rows, send, place, back, lift_wide = pl.pallas_call(
        volume_kernel,
        out_shape=[
            array(NB + 1, dtype=jnp.int32),
            array(SLOTS, BLK),
            array(NB, 6, NPAD, BLK),
            array(4 * NF, BLK, dtype=jnp.int32),
            array(NF, BLK, dtype=jnp.int32),
            array(4 * NF, BLK, dtype=jnp.int32),
            array(BLK, KROWS, dtype=BF16),
            array(KLIFT, 2 * BLK, dtype=BF16),
        ],
        in_specs=[SMEM] * 2 + [VMEM] * 7,
        out_specs=[SMEM] + [VMEM] * 7,
        scratch_shapes=[
            pltpu.VMEM((BLK, BLK), F32),
            pltpu.VMEM((6, NPAD, NB * BLK), F32),
            pltpu.SMEM((5, NB), jnp.int32),
        ],
        compiler_params=PARAMS,
        cost_estimate=cost(10**9, 4 * 10**6),
        name="volume",
    )(neighbor.reshape(SLOTS), ranks, codes, slots, table, fields, metric, derivative, lift)
    rows = rows.reshape(FSLOTS)
    rate, start, table, *out = pl.pallas_call(
        full_kernel,
        out_shape=[array(6, NP, NB * BLK), state_shape, array(FTAB, BLK)] + message(NF * BFB) + [array(SLOTS, BLK)],
        in_specs=[SMEM] * 3 + [VMEM] * 12,
        out_specs=[HBM] + [VMEM] * 7,
        scratch_shapes=[
            pltpu.VMEM((NB, 6, NP, BLK), F32),
            pltpu.VMEM((NB, 6, NPAD, BLK), F32),
            pltpu.SemaphoreType.DMA((NB,)),
        ],
        input_output_aliases={4: 7},
        compiler_params=PARAMS,
        cost_estimate=cost(10**9, 4 * 10**6),
        name="full",
    )(slots, send, meta, table, outer, curl, normals, face_scale, medium, front, lift_wide, *received)
    state = start
    for step in range(3):
        received = exchange(out)
        outer, curl = pl.pallas_call(
            fine_volume_kernel,
            out_shape=[array(FSLOTS + 8, BLK), state_shape],
            in_specs=[SMEM] * 2 + [VMEM] * 4,
            out_specs=[VMEM] * 2,
            compiler_params=PARAMS,
            cost_estimate=cost(10**9, 2 * 10**6),
            name="fine_volume",
        )(rows, meta, table, state, metric, back)
        geometry = (normals, face_scale, medium)
        if step < 2:
            state, table, *out = pl.pallas_call(
                fine_kernel,
                out_shape=[state_shape, array(FTAB, BLK)] + message(NF * BFB) + [array(FSLOTS + 8, BLK)],
                in_specs=[SMEM] * 3 + [VMEM] * 14,
                out_specs=[VMEM] * 7,
                input_output_aliases={6: 6},
                compiler_params=PARAMS,
                cost_estimate=cost(10**9, 2 * 10**6),
                name="fine",
            )(place, send, meta, state, start, table, outer, curl, *geometry, front, lift_wide, *received)
    return pl.pallas_call(
        last_kernel,
        out_shape=[array(6, NP, NB * BLK), array(FSLOTS + 8, BLK)],
        in_specs=[SMEM] * 2 + [VMEM] * 13 + [HBM],
        out_specs=[HBM, VMEM],
        scratch_shapes=[pltpu.VMEM((NF, 6, NP, BLK), F32), pltpu.SemaphoreType.DMA((NF,))],
        input_output_aliases={15: 0, 5: 1},
        compiler_params=PARAMS,
        cost_estimate=cost(10**9, 2 * 10**6),
        name="last",
    )(place, meta, state, start, table, outer, curl, *geometry, lift_wide, *received, rate)[0]


def solution(mesh):
    in_specs = (
        P(None, None, ("px", "py")),
        P(None, None, ("px", "py")),
        P(None, None, ("px", "py")),
        P(None, ("px", "py")),
        P(("px", "py")),
        P(),
        P(),
        P(),
        P("px", "py", None),
        P(),
    )
    out_specs = P(None, None, ("px", "py"))
    return jax.shard_map(shards, mesh=mesh, in_specs=in_specs, out_specs=out_specs, check_vma=False)
```

```python
import jax
import jax.numpy as jnp
from jax import lax
from jax.experimental import pallas as pl
from jax.experimental.pallas import tpu as pltpu
from jax.sharding import PartitionSpec as P

F32 = jnp.float32
BF16 = jnp.bfloat16
BLK = 128
BFB = 16
NB = 8
NF = 4
NP = 35
NPAD = 40
KLIFT = 48
KROWS = 128
FPAD = 16
STEP = 0.05
SLOTS = 4 * NB * BLK
FSLOTS = 4 * NF * BLK
FRECV = 4 * NF * BFB
ZROW = FSLOTS
TAB = SLOTS + 4 * NB * BFB
FTAB = ZROW + 8
TRASH = FSLOTS
VMEM_LIMIT = 16 * 1024 * 1024


def split(x):
    hi = x.astype(BF16)
    lo = (x - hi.astype(F32)).astype(BF16)
    return hi, lo


def node_products(matrix, nodal):
    wide = jnp.concatenate(nodal, axis=1)
    hi = wide.astype(BF16).astype(F32)
    zero = jnp.zeros((KROWS - 3 * NPAD, 6 * BLK), F32)
    wide = jnp.concatenate([hi, wide - hi, hi, zero], axis=0).astype(BF16)
    return jnp.dot(matrix, wide, preferred_element_type=F32)


def stacked(matrix):
    hi = matrix.astype(BF16).astype(F32)
    return (hi + pltpu.roll(hi, NPAD, 1) + pltpu.roll(matrix - hi, 2 * NPAD, 1)).astype(BF16)


def store_traces(products, table, stride, base):
    for f in range(4):
        rows = products[f * FPAD : (f + 1) * FPAD]
        parts = [rows[:, c * BLK : (c + 1) * BLK] for c in range(6)]
        tile = jnp.concatenate(parts + [jnp.zeros((BLK - 6 * FPAD, BLK), F32)], axis=0)
        table[pl.ds(f * stride + base, BLK), :] = tile.T


def curls(products, metric, lanes):
    def nodal(a, c):
        return products[a * NPAD : (a + 1) * NPAD, c * BLK : (c + 1) * BLK]

    rows = [[metric[i, a : a + 1, lanes] for a in range(3)] for i in range(3)]

    def grad(i, c):
        return rows[i][0] * nodal(0, c) + rows[i][1] * nodal(1, c) + rows[i][2] * nodal(2, c)

    curl_h = [grad(1, 5) - grad(2, 4), grad(2, 3) - grad(0, 5), grad(0, 4) - grad(1, 3)]
    curl_e = [grad(1, 2) - grad(2, 1), grad(2, 0) - grad(0, 2), grad(0, 1) - grad(1, 0)]
    return curl_h + curl_e


def cross(n, v):
    return [n[1] * v[2] - n[2] * v[1], n[2] * v[0] - n[0] * v[2], n[0] * v[1] - n[1] * v[0]]


def lifted_flux(outer, table, stride, base, normals, scale, lanes, lift):
    faces = [[], [], [], [], [], []]
    for f in range(4):
        at = pl.ds(f * stride + base, BLK)
        jump = (outer[at, :] - table[at, :]).T
        de = [jump[c * FPAD : (c + 1) * FPAD] for c in range(3)]
        dh = [jump[c * FPAD : (c + 1) * FPAD] for c in range(3, 6)]
        n = [normals[i, f : f + 1, lanes] for i in range(3)]
        half = 0.5 * scale[f : f + 1, lanes]
        dot_e = n[0] * de[0] + n[1] * de[1] + n[2] * de[2]
        dot_h = n[0] * dh[0] + n[1] * dh[1] + n[2] * dh[2]
        nh = cross(n, dh)
        ne = cross(n, de)
        for i in range(3):
            faces[i].append((nh[i] + de[i] - dot_e * n[i]) * half)
            faces[3 + i].append((dh[i] - dot_h * n[i] - ne[i]) * half)
    wide = jnp.concatenate([jnp.concatenate(x, axis=0) for x in faces], axis=1)
    hi, lo = split(wide)
    out = jnp.dot(lift[:, : 12 * FPAD], jnp.concatenate([hi, lo, hi], axis=0), preferred_element_type=F32)
    return [out[:NPAD, c * BLK : (c + 1) * BLK] for c in range(6)]


def tendency(curl, lifted, medium, lanes):
    inverse = 1.0 / medium[:, lanes]
    electric = [(curl[c] + lifted[c]) * inverse for c in range(3)]
    return electric + [lifted[c] - curl[c] for c in range(3, 6)]


def copy_rows(index, source, target, base):
    for r in range(BLK):
        target[pl.ds(base + r, 1), :] = source[pl.ds(index[base + r], 1), :]


def send_rows(index, table, outs):
    for d in range(4):
        for i in range(NF):
            for w in range(BFB):
                r = i * BFB + w
                outs[d][r : r + 1, :] = table[pl.ds(index[i, d * BFB + w], 1), :]


def pad_nodes(fields, padded, lo, hi):
    for c in range(6):
        padded[c, 32:NPAD, lo:hi] = jnp.zeros((NPAD - 32, hi - lo), F32)
        padded[c, 0:NP, lo:hi] = fields[c, :, lo:hi]


def block_lanes(b):
    return pl.ds(b * BLK if isinstance(b, int) else pl.multiple_of(b * BLK, BLK), BLK)


def each(count, body):
    for b in range(count):
        body(b)


def compact_rows(code, rank):
    block = (code >> 7) & 7
    place = jnp.full_like(code, NB)
    for b in range(NB):
        place = jnp.where(block == b, rank[0, b], place)
    row = (code >> 10) * (NF * BLK) + place * BLK + (code & 127)
    return jnp.where((code < SLOTS) & (place < NF), row, ZROW)


def find_slots(codes, wide, index):
    wide[...] = jnp.zeros_like(wide)
    wide[0 : 4 * NB, :] = codes[...].astype(F32)
    columns = wide[...].T
    lane = lax.broadcasted_iota(jnp.int32, (BLK, BLK), 1)
    element = lax.broadcasted_iota(jnp.int32, (BLK, BLK), 0).astype(F32)
    for b in range(NB):
        wanted = (SLOTS + (lane >> 4) * (NB * BFB) + b * BFB + (lane & 15)).astype(F32)
        found = jnp.zeros((BLK, BLK), F32)
        for f in range(4):
            column = columns[:, f * NB + b : f * NB + b + 1]
            found += jnp.where(column == wanted, element + (f * NB + b) * BLK, 0.0)
        index[b : b + 1, :] = jnp.sum(found, axis=0, keepdims=True).astype(jnp.int32)


def first_kernel(
    ranks, code_rows, fields, interp, slots, table, front, out0, out1, out2, out3,
    padded, raw, code_buf, interp_buf, wide, index, sem,
):
    half = NB * BLK // 2
    copies = [
        pltpu.make_async_copy(code_rows, code_buf, sem.at[0]),
        pltpu.make_async_copy(interp, interp_buf, sem.at[1]),
    ] + [
        pltpu.make_async_copy(
            fields.at[:, :, h * half : (h + 1) * half], raw.at[:, :, h * half : (h + 1) * half], sem.at[2 + h]
        )
        for h in range(2)
    ]
    for copy in copies:
        copy.start()
    table[SLOTS:TAB, :] = jnp.zeros((TAB - SLOTS, BLK), F32)
    copies[0].wait()
    find_slots(code_buf, wide, slots)
    to_scalar = pltpu.make_async_copy(slots, index, sem.at[4])
    to_scalar.start()
    copies[1].wait()
    wide[...] = jnp.zeros_like(wide)
    for f in range(4):
        for m in range(15):
            wide[f * FPAD + m : f * FPAD + m + 1, 0:NP] = interp_buf[m, f : f + 1, :]
    front[...] = stacked(wide[0 : 4 * FPAD, :])
    for h in range(2):
        copies[2 + h].wait()
        pad_nodes(raw, padded, h * half, (h + 1) * half)

        def traces(i, h=h):
            b = i + h * NB // 2
            lanes = block_lanes(b)
            products = node_products(front[...], [padded[c, :, lanes] for c in range(6)])
            store_traces(products, table, NB * BLK, b * BLK)

        each(NB // 2, traces)
    to_scalar.wait()
    for d, out in enumerate((out0, out1, out2, out3)):
        for b in range(NB):
            for w in range(BFB):
                out[b * BFB + w : b * BFB + w + 1, :] = table[pl.ds(index[b, d * BFB + w], 1), :]


def volume_kernel(
    codes, rank, code_rows, slots, table, fields, metric, derivative, lift,
    meta, outer, curl, rows, send, place, back, lift_wide, wide, padded, order,
):
    count = 0
    for x in range(5):
        for b in range(NB):
            order[x, rank[x, b]] = b
    for b in range(NB):
        meta[b] = order[0, b]
        count += rank[5, b]
    meta[NB] = count
    for f in range(4):
        for i in range(NF):
            rows[f * NF + i : f * NF + i + 1, :] = code_rows[pl.ds(f * NB + meta[i], 1), :]
    rows[...] = compact_rows(rows[...], rank)
    for i in range(NF):
        slot = slots[pl.ds(meta[i], 1), :]
        send[i : i + 1, :] = (slot >> 10) * (NF * BLK) + i * BLK + (slot & 127)
    for d in range(4):
        for i in range(NF):
            b = order[1 + d, i]
            own = rank[0, b]
            slot = slots[pl.ds(b, 1), :]
            row = (slot >> 10) * (NF * BLK) + own * BLK + (slot & 127)
            place[d * NF + i : d * NF + i + 1, :] = jnp.where(own < NF, row, TRASH)
    wide[...] = jnp.zeros_like(wide)
    for a in range(3):
        wide[a * NPAD : a * NPAD + NP, 0:NP] = derivative[a]
    back[...] = stacked(wide[...])
    wide[0:KLIFT, :] = jnp.zeros((KLIFT, BLK), F32)
    wide[0:NP, 0:60] = lift[...]
    flat = wide[0:KLIFT, :]
    lane = lax.broadcasted_iota(jnp.int32, (KLIFT, BLK), 1)
    face_major = jnp.where(lane < 15, flat, 0.0)
    for f in range(1, 4):
        inside = (lane >= f * FPAD) & (lane < f * FPAD + 15)
        face_major = jnp.where(inside, pltpu.roll(flat, f, 1), face_major)
    hi = face_major.astype(BF16).astype(F32)
    lift_wide[:, 0:BLK] = (hi + pltpu.roll(hi, 4 * FPAD, 1)).astype(BF16)
    lift_wide[:, BLK : 2 * BLK] = (face_major - hi).astype(BF16)
    pad_nodes(fields, padded, 0, NB * BLK)

    def block(b):
        lanes = block_lanes(b)
        for f in range(4):
            copy_rows(codes, table, outer, f * NB * BLK + b * BLK)
        products = node_products(back[...], [padded[c, :, lanes] for c in range(6)])
        for c, value in enumerate(curls(products, metric, lanes)):
            curl[b, c] = value

    each(NB, block)


def start_rate(b, outer, table, curl, normals, scale, medium, lift):
    lanes = block_lanes(b)
    lifted = lifted_flux(
        outer, table, NB * BLK, pl.multiple_of(b * BLK, BLK), normals, scale, lanes, lift
    )
    return tendency([curl[b, c] for c in range(6)], lifted, medium, lanes)


def full_kernel(
    slots, send, meta, table, outer_in, curl, normals, scale, medium, front, lift, in0, in1, in2, in3,
    start, state, fine_table, out0, out1, out2, out3, outer,
):
    for d, got in enumerate((in0, in1, in2, in3)):
        for b in range(NB):
            for w in range(BFB):
                outer[pl.ds(slots[b, d * BFB + w], 1), :] = got[b * BFB + w : b * BFB + w + 1, :]
    fine_table[ZROW : ZROW + 8, :] = jnp.zeros((8, BLK), F32)
    for i in range(NF):
        value = start_rate(meta[i], outer, table, curl, normals, scale, medium, lift)
        keep = i < meta[NB]
        kept = [jnp.where(keep, x, 0.0) for x in value]
        for c in range(6):
            start[i, c] = value[c]
            state[i, c] = kept[c]
        store_traces(node_products(front[...], kept), fine_table, NF * BLK, i * BLK)
    send_rows(send, fine_table, (out0, out1, out2, out3))


def coarse_kernel(
    codes, meta, table, state, metric, back, all_outer, all_table, all_curl, normals, scale, medium, lift,
    outer, curl, rate, result, sem,
):
    copies = []
    for j in range(NB - NF):
        b = meta[NF + j]
        value = start_rate(b, all_outer, all_table, all_curl, normals, scale, medium, lift)
        for c in range(6):
            result[j, c] = value[c][:NP]
        copies.append(pltpu.make_async_copy(result.at[j], rate.at[:, :, block_lanes(b)], sem.at[j]))
        copies[-1].start()
    fine_volume_kernel(codes, meta, table, state, metric, back, outer, curl)
    for copy in copies:
        copy.wait()


def fine_volume_kernel(codes, meta, table, state, metric, back, outer, curl):
    def block(i):
        for f in range(4):
            copy_rows(codes, table, outer, f * NF * BLK + i * BLK)
        products = node_products(back[...], [state[i, c] for c in range(6)])
        for c, value in enumerate(curls(products, metric, block_lanes(meta[i]))):
            curl[i, c] = value

    each(NF, block)


def fine_update(
    place, meta, state, start, table, outer, curl, normals, scale, medium, lift, ins, emit
):
    for d, got in enumerate(ins):
        for i in range(NF):
            for w in range(BFB):
                r = i * BFB + w
                outer[pl.ds(place[d * NF + i, d * BFB + w], 1), :] = got[r : r + 1, :]
    def block(i):
        lanes = block_lanes(meta[i])
        lifted = lifted_flux(outer, table, NF * BLK, i * BLK, normals, scale, lanes, lift)
        value = tendency([curl[i, c] for c in range(6)], lifted, medium, lanes)
        keep = i < meta[NB]
        emit(i, [
            jnp.where(keep, state[i, c] + start[i, c] + STEP * value[c], 0.0) for c in range(6)
        ])

    each(NF, block)


def fine_kernel(
    place, send, meta, state, start, table, outer_in, curl, normals, scale, medium, front, lift,
    in0, in1, in2, in3, new_state, new_table, out0, out1, out2, out3, outer,
):
    def emit(i, value):
        for c in range(6):
            new_state[i, c] = value[c]
        store_traces(node_products(front[...], value), new_table, NF * BLK, i * BLK)

    new_table[ZROW : ZROW + 8, :] = jnp.zeros((8, BLK), F32)
    fine_update(
        place, meta, state, start, table, outer, curl, normals, scale, medium, lift,
        (in0, in1, in2, in3), emit,
    )
    send_rows(send, new_table, (out0, out1, out2, out3))


def last_kernel(
    place, meta, state, start, table, outer_in, curl, normals, scale, medium, lift,
    in0, in1, in2, in3, rate_in, rate, outer, result, sem,
):
    def copy(i):
        return pltpu.make_async_copy(result.at[i], rate.at[:, :, block_lanes(meta[i])], sem.at[i])

    def emit(i, value):
        keep = i < meta[NB]
        for c in range(6):
            result[i, c] = jnp.where(keep, value[c] * 0.25, start[i, c])[:NP]
        copy(i).start()

    fine_update(
        place, meta, state, start, table, outer, curl, normals, scale, medium, lift,
        (in0, in1, in2, in3), emit,
    )
    for i in range(NF):
        copy(i).wait()


def fine_plan(levels):
    padded = jnp.pad(levels, ((1, 1), (1, 1), (0, 0)))
    near = lax.dynamic_slice(padded, (lax.axis_index("px"), lax.axis_index("py"), 0), (3, 3, NB))
    fine = (jnp.stack([near[1, 1], near[0, 1], near[2, 1], near[1, 0], near[1, 2]]) > 0).astype(jnp.int32)
    before = (jnp.arange(NB)[None, :] < jnp.arange(NB)[:, None]).astype(jnp.int32)
    fine_before = jnp.sum(fine[:, None, :] * before[None], axis=2)
    coarse_before = jnp.sum((1 - fine[:, None, :]) * before[None], axis=2)
    count = jnp.sum(fine, axis=1, keepdims=True)
    rank = jnp.where(fine > 0, fine_before, count + coarse_before)
    return jnp.concatenate([rank, fine[:1]])


VMEM = pl.BlockSpec(memory_space=pltpu.VMEM)
SMEM = pl.BlockSpec(memory_space=pltpu.SMEM)
HBM = pl.BlockSpec(memory_space=pltpu.HBM)
PARAMS = pltpu.CompilerParams(vmem_limit_bytes=VMEM_LIMIT)


def cost(flops, size):
    return pl.CostEstimate(flops=flops, bytes_accessed=size, transcendentals=0)


def shards(
    fields, metric, normals, face_scale, permittivity, derivative, face_interp, lift, neighbor, levels
):
    codes = neighbor.reshape(4 * NB, BLK)
    medium = permittivity.reshape(1, NB * BLK)

    def exchange(out):
        def ways(axis):
            count = lax.axis_size(axis)
            return [(i, i + 1) for i in range(count - 1)], [(i + 1, i) for i in range(count - 1)]

        x_up, x_down = ways("px")
        y_up, y_down = ways("py")
        return (
            lax.ppermute(out[1], "px", x_up),
            lax.ppermute(out[0], "px", x_down),
            lax.ppermute(out[3], "py", y_up),
            lax.ppermute(out[2], "py", y_down),
        )

    def message(rows_of):
        return [jax.ShapeDtypeStruct((rows_of, BLK), F32)] * 4

    def array(*shape, dtype=F32):
        return jax.ShapeDtypeStruct(shape, dtype)

    state_shape = array(NF, 6, NPAD, BLK)
    ranks = fine_plan(levels)
    slots, table, front, *out = pl.pallas_call(
        first_kernel,
        out_shape=[
            array(NB, BLK, dtype=jnp.int32),
            array(TAB, BLK),
            array(4 * FPAD, KROWS, dtype=BF16),
        ] + message(NB * BFB),
        in_specs=[VMEM] + [HBM] * 3,
        out_specs=[VMEM] * 7,
        scratch_shapes=[
            pltpu.VMEM((6, NPAD, NB * BLK), F32),
            pltpu.VMEM((6, NP, NB * BLK), F32),
            pltpu.VMEM((4 * NB, BLK), jnp.int32),
            pltpu.VMEM((15, 4, NP), F32),
            pltpu.VMEM((BLK, BLK), F32),
            pltpu.SMEM((NB, BLK), jnp.int32),
            pltpu.SemaphoreType.DMA((5,)),
        ],
        compiler_params=PARAMS,
        cost_estimate=cost(10**9, 2 * 10**6),
        name="border",
    )(ranks, codes, fields, face_interp.transpose(1, 0, 2))
    received = exchange(out)
    meta, outer, curl, rows, send, place, back, lift_wide = pl.pallas_call(
        volume_kernel,
        out_shape=[
            array(NB + 1, dtype=jnp.int32),
            array(SLOTS, BLK),
            array(NB, 6, NPAD, BLK),
            array(4 * NF, BLK, dtype=jnp.int32),
            array(NF, BLK, dtype=jnp.int32),
            array(4 * NF, BLK, dtype=jnp.int32),
            array(BLK, KROWS, dtype=BF16),
            array(KLIFT, 2 * BLK, dtype=BF16),
        ],
        in_specs=[SMEM] * 2 + [VMEM] * 7,
        out_specs=[SMEM] + [VMEM] * 7,
        scratch_shapes=[
            pltpu.VMEM((BLK, BLK), F32),
            pltpu.VMEM((6, NPAD, NB * BLK), F32),
            pltpu.SMEM((5, NB), jnp.int32),
        ],
        compiler_params=PARAMS,
        cost_estimate=cost(10**9, 4 * 10**6),
        name="volume",
    )(neighbor.reshape(SLOTS), ranks, codes, slots, table, fields, metric, derivative, lift)
    rows = rows.reshape(FSLOTS)
    geometry = (normals, face_scale, medium)
    all_table, all_curl = table, curl
    start, state, table, *out, all_outer = pl.pallas_call(
        full_kernel,
        out_shape=[state_shape] * 2 + [array(FTAB, BLK)] + message(NF * BFB) + [array(SLOTS, BLK)],
        in_specs=[SMEM] * 3 + [VMEM] * 12,
        out_specs=[VMEM] * 8,
        input_output_aliases={4: 7},
        compiler_params=PARAMS,
        cost_estimate=cost(10**9, 4 * 10**6),
        name="full",
    )(slots, send, meta, all_table, outer, curl, *geometry, front, lift_wide, *received)
    for step in range(3):
        received = exchange(out)
        volume_shape = [array(FSLOTS + 8, BLK), state_shape]
        volume_args = (rows, meta, table, state, metric, back)
        if step == 0:
            outer, curl, rate = pl.pallas_call(
                coarse_kernel,
                out_shape=volume_shape + [array(6, NP, NB * BLK)],
                in_specs=[SMEM] * 2 + [VMEM] * 11,
                out_specs=[VMEM] * 2 + [HBM],
                scratch_shapes=[
                    pltpu.VMEM((NB - NF, 6, NP, BLK), F32),
                    pltpu.SemaphoreType.DMA((NB - NF,)),
                ],
                compiler_params=PARAMS,
                cost_estimate=cost(10**9, 2 * 10**6),
                name="coarse",
            )(*volume_args, all_outer, all_table, all_curl, *geometry, lift_wide)
        else:
            outer, curl = pl.pallas_call(
                fine_volume_kernel,
                out_shape=volume_shape,
                in_specs=[SMEM] * 2 + [VMEM] * 4,
                out_specs=[VMEM] * 2,
                compiler_params=PARAMS,
                cost_estimate=cost(10**9, 2 * 10**6),
                name="fine_volume",
            )(*volume_args)
        if step < 2:
            state, table, *out = pl.pallas_call(
                fine_kernel,
                out_shape=[state_shape, array(FTAB, BLK)] + message(NF * BFB) + [array(FSLOTS + 8, BLK)],
                in_specs=[SMEM] * 3 + [VMEM] * 14,
                out_specs=[VMEM] * 7,
                input_output_aliases={6: 6},
                compiler_params=PARAMS,
                cost_estimate=cost(10**9, 2 * 10**6),
                name="fine",
            )(place, send, meta, state, start, table, outer, curl, *geometry, front, lift_wide, *received)
    return pl.pallas_call(
        last_kernel,
        out_shape=[array(6, NP, NB * BLK), array(FSLOTS + 8, BLK)],
        in_specs=[SMEM] * 2 + [VMEM] * 13 + [HBM],
        out_specs=[HBM, VMEM],
        scratch_shapes=[pltpu.VMEM((NF, 6, NP, BLK), F32), pltpu.SemaphoreType.DMA((NF,))],
        input_output_aliases={15: 0, 5: 1},
        compiler_params=PARAMS,
        cost_estimate=cost(10**9, 2 * 10**6),
        name="last",
    )(place, meta, state, start, table, outer, curl, *geometry, lift_wide, *received, rate)[0]


def solution(mesh):
    in_specs = (
        P(None, None, ("px", "py")),
        P(None, None, ("px", "py")),
        P(None, None, ("px", "py")),
        P(None, ("px", "py")),
        P(("px", "py")),
        P(),
        P(),
        P(),
        P("px", "py", None),
        P(),
    )
    out_specs = P(None, None, ("px", "py"))
    return jax.shard_map(shards, mesh=mesh, in_specs=in_specs, out_specs=out_specs, check_vma=False)
```
